768 devices in a mesh: gx: 24 (over z_lo, x), gy: 32 (over z_hi, y, core).
Axes of the slice: x: 4, y: 8, z: 12 (z_hi: 2, z_lo: 6; z = z_hi * 6 + z_lo), core: 2. Of those that a mesh axis runs over, the one named last changes fastest.
Arguments:
- positions: float32 [3, 6291456], P(None, ('gx', 'gy')), may hold values from -6 to 6
- velocities: float32 [3, 6291456], P(None, ('gx', 'gy')), may hold values from -4 to 4
- masses: float32 [6291456], P(('gx', 'gy')), may hold values from 0.005 to 0.05
- long_kick: float32 [3, 6291456], P(None, ('gx', 'gy')), may hold values from -3 to 3
- leaf_lists: int32 [8, 49152], P(None, ('gx', 'gy')), may hold values from 0 to 135, as said below
- ghost_ids: int32 [6144], P(('gx', 'gy')), may hold values from 0 to 63, as said below
- leaf_counts: int32 [768], P(('gx', 'gy')), may hold values from 1 to 64, as said below
Outputs:
- new_positions: float32 [3, 6291456], P(None, ('gx', 'gy'))
- new_velocities: float32 [3, 6291456], P(None, ('gx', 'gy'))
The draws below stay inside these ranges and needn't reach their ends.
Inputs may be any that keep to these rules, and one draw needn't show every extreme that they name: leaf_counts of a domain is at least 1; the counts of domains (i, j) and (i, j + 16) for j below 16 sum to at most 80, and some pair reaches it with one count equal to 64. `leaf_lists`: every entry below 64 is below the count of its domain; entries from 64 on name pool ghost leaves. `ghost_ids`: each id is below the count of its domain; ids may repeat.
All inputs are finite; a program needn't handle non-finite values.
Results may differ from the reference program's by a relative error of at most 0.00011.
Values sent between devices are 32-bit elements; how exact they have to be, the bound alone decides.
No kernel may reach another device: no remote copies, remote signals or barrier semaphores. Data moves between devices by JAX's collectives and lax.ppermute only.
A program may use at most 32 MiB of HBM per device.

```python
import math
import jax
import jax.numpy as jnp
from jax import lax

LEAF = 128
NEIGHBOURS = 8
LEAVES = 64
GHOSTS = 8
SUBCYCLES = 4
BAL = 40
SLABS = 24
COLUMNS = 32
DOMAINS = 768
PARTICLES = 6291456


def pair_counts(key):
    base = jax.random.fold_in(key, 7)
    first_key, second_key = jax.random.split(base)
    half = COLUMNS // 2
    totals = jax.random.randint(first_key, (SLABS, half), 4, 2 * BAL + 1)
    totals = totals.at[0, 0].set(2 * BAL)
    lowest = jnp.maximum(1, totals - LEAVES)
    highest = jnp.minimum(LEAVES, totals - 1)
    first = jax.random.randint(second_key, (SLABS, half), lowest, highest + 1)
    first = first.at[0, 0].set(LEAVES)
    second = totals - first
    return jnp.concatenate([first, second], axis=1).reshape(-1).astype(jnp.int32)


def draw_leaf_counts(key, part):
    return pair_counts(key)


def draw_leaf_lists(key, part):
    counts = pair_counts(key)
    per_leaf = jnp.repeat(counts, LEAVES, total_repeat_length=DOMAINS * LEAVES)
    base = jax.random.fold_in(key, 11)
    own_key, ghost_key, pick_key = jax.random.split(base, 3)
    shape = (NEIGHBOURS, DOMAINS * LEAVES)
    own_pick = jax.random.randint(own_key, shape, 0, jnp.broadcast_to(per_leaf[None, :], shape))
    ghost_pick = LEAVES + jax.random.randint(ghost_key, shape, 0, 9 * GHOSTS)
    which = jax.random.randint(pick_key, shape, 0, 2)
    return jnp.where(which == 1, ghost_pick, own_pick).astype(jnp.int32)


def draw_ghost_ids(key, part):
    counts = pair_counts(key)
    per_ghost = jnp.repeat(counts, GHOSTS, total_repeat_length=DOMAINS * GHOSTS)
    base = jax.random.fold_in(key, 13)
    return jax.random.randint(base, (DOMAINS * GHOSTS,), 0, per_ghost).astype(jnp.int32)


def levels(key, shape, cuts, low, largest):
    def one(dim, blocks):
        steps = jax.random.uniform(jax.random.fold_in(jax.random.fold_in(key, 6), dim), (blocks,), jnp.float32, low / len(cuts), largest / len(cuts))
        return jnp.repeat(jnp.exp(steps), shape[dim] // blocks).reshape((-1,) + (1,) * (len(shape) - dim - 1))

    gain = one(*cuts[0])
    for cut in cuts[1:]:
        gain = gain * one(*cut)
    return gain


def scatter_about(rng, extent, deviation, limit, cuts=(), held_as=jnp.bfloat16):
    level = levels(rng, extent, cuts, -0.22, 0.18) if cuts else 1.0
    result = jax.random.normal(rng, extent, jnp.float32) * deviation * level
    return jnp.minimum(jnp.maximum(result, -limit), limit).astype(held_as)


def setup_inputs(seed: int = 0) -> dict:
    key_list = jax.random.split(jax.random.key(seed), 8)
    return {
        "positions": scatter_about(key_list[0], (3, PARTICLES), 1.0, 6.0, ((1, 768),), jnp.float32),
        "velocities": scatter_about(key_list[1], (3, PARTICLES), 0.5, 4.0, ((1, 768),), jnp.float32),
        "masses": jnp.clip(jnp.exp(math.log(0.05) - 2.3025851 * jax.random.uniform(key_list[2], (PARTICLES,), jnp.float32) ** levels(key_list[2], (PARTICLES,), ((0, 768),), -0.2, 0.2)), 0.005, 0.05),
        "long_kick": scatter_about(key_list[3], (3, PARTICLES), 0.3, 3.0, ((1, 768),), jnp.float32),
        "leaf_lists": draw_leaf_lists(jax.random.fold_in(key_list[7], 71), 0),
        "ghost_ids": draw_ghost_ids(jax.random.fold_in(key_list[7], 71), 0),
        "leaf_counts": draw_leaf_counts(jax.random.fold_in(key_list[7], 71), 0),
    }


soften_sq = 0.04
cutoff_sq = 9.0
time_step = 0.5

def pair_accel(targets, sources):
    offsets = sources[:3, :, None, :] - targets[:, :, :, None]
    distance = lax.optimization_barrier(jnp.sum(offsets * offsets, axis=0))
    tapers = jnp.square(jnp.maximum(1.0 - distance / cutoff_sq, 0.0))
    inverse = lax.rsqrt(distance + soften_sq)
    weight = sources[3][:, None, :] * tapers * inverse * inverse * inverse
    return lax.optimization_barrier(jnp.sum(offsets * weight[None], axis=3))

def accumulate(targets, operands):

    def add_tile(index, summed):
        sources = lax.dynamic_index_in_dim(operands, index, 1, keepdims=False)
        return summed + pair_accel(targets, sources)
    return lax.fori_loop(0, operands.shape[1], add_tile, jnp.zeros(targets.shape, targets.dtype))

def gather_pool(pool_rows, list_rows):
    return jnp.take(pool_rows, list_rows, axis=1)

def reference(positions, velocities, masses, long_kick, leaf_lists, ghost_ids, leaf_counts):
    places = jnp.moveaxis(positions.reshape(3, SLABS, COLUMNS, LEAVES, LEAF), 0, 2)
    speeds = jnp.moveaxis(velocities.reshape(3, SLABS, COLUMNS, LEAVES, LEAF), 0, 2)
    kicks = jnp.moveaxis(long_kick.reshape(3, SLABS, COLUMNS, LEAVES, LEAF), 0, 2)
    mass_rows = masses.reshape(SLABS, COLUMNS, 1, LEAVES, LEAF)
    lists = jnp.moveaxis(leaf_lists.reshape(NEIGHBOURS, SLABS, COLUMNS, LEAVES), 0, 2)
    ghosts = ghost_ids.reshape(SLABS, COLUMNS, 1, GHOSTS, 1)
    ghosts = jnp.broadcast_to(ghosts, (SLABS, COLUMNS, 4, GHOSTS, LEAF))
    counts = leaf_counts.reshape(SLABS, COLUMNS, 1, 1, 1)
    live = jnp.arange(LEAVES).astype(jnp.int32)[None, None, None, :, None] < counts
    for subcycle in range(SUBCYCLES):
        own_rows = jnp.concatenate([places, mass_rows], axis=2)
        chosen = jnp.take_along_axis(own_rows, ghosts, axis=3)
        parts = [own_rows]
        for shift_x in (-1, 0, 1):
            for shift_y in (-1, 0, 1):
                parts.append(jnp.roll(jnp.roll(chosen, -shift_x, axis=0), -shift_y, axis=1))
        pool = jnp.concatenate(parts, axis=3)
        operands = jax.vmap(jax.vmap(gather_pool))(pool, lists)

        def slab_accel(items):
            return jax.vmap(accumulate)(items[0], items[1])
        accel = lax.map(slab_accel, (places, operands))
        speeds = jnp.where(live, speeds + time_step * (accel + kicks), speeds)
        places = jnp.where(live, places + time_step * speeds, places)
    new_positions = jnp.moveaxis(places, 2, 0).reshape(3, -1)
    new_velocities = jnp.moveaxis(speeds, 2, 0).reshape(3, -1)
    return (new_positions, new_velocities)
```

```python
import jax
import jax.numpy as jnp
from jax import lax
from jax.experimental import pallas as pl
from jax.experimental.pallas import tpu as pltpu
from jax.sharding import PartitionSpec as P

SUBCYCLES = 4
LEAF = 128
LEAVES = 64
GHOSTS = 8
NEIGHBOURS = 8
POOL = LEAVES + 9 * GHOSTS
FEATURES = 32
SUMS = 16
GROUP = 4
UNROLL = 8

soften_sq = 0.04
cutoff_sq = 9.0
time_step = 0.5

f32, bf16 = jnp.float32, jnp.bfloat16


def three_parts(value):
    first = value.astype(bf16).astype(f32)
    rest = value - first
    second = rest.astype(bf16).astype(f32)
    return first, second, (rest - second).astype(bf16).astype(f32)


def norm_parts(record, more=0.0):
    square = record * record
    return three_parts(square[0:1] + square[1:2] + square[2:3] + more)


def with_row(parts, row):
    last = lax.broadcasted_iota(jnp.int32, parts.shape, 0) == 3
    return jnp.where(last, jnp.broadcast_to(row, parts.shape), parts)


def source_features(record):
    a, b, c = three_parts(record)
    n1, n2, n3 = norm_parts(record)
    one = jnp.ones_like(n1)
    zero = jnp.zeros((8, LEAF), f32)
    return jnp.concatenate(
        [
            with_row(a, n1),
            with_row(a, n2),
            with_row(b, n3),
            with_row(b, one),
            with_row(a, one),
            with_row(c, one),
            zero,
        ],
        axis=0,
    )


def target_features(record):
    a, b, c = three_parts(record * -2.0)
    n1, n2, n3 = norm_parts(record, soften_sq)
    one = jnp.ones_like(n1)
    zero = jnp.zeros((8, LEAF), f32)
    return jnp.concatenate(
        [
            with_row(a, one),
            with_row(b, one),
            with_row(a, one),
            with_row(b, n1),
            with_row(c, n2),
            with_row(a, n3),
            zero,
        ],
        axis=0,
    )


def moment_rows(record):
    mass = jnp.broadcast_to(record[3:4], record.shape)
    a, b, c = three_parts(with_row(record, jnp.ones((1, LEAF), f32)) * mass)
    return jnp.concatenate([a, b, c, jnp.zeros_like(a)], axis=0).astype(bf16)


def enter(sources, moments, slot, record):
    features = source_features(record)
    blank = jnp.zeros((LEAF - FEATURES, LEAF), f32)
    sources[slot] = jnp.concatenate([features, blank], axis=0).T.astype(bf16)
    moments[slot] = moment_rows(record)


def enter_all(sources, moments, rows, slot_of, many):
    def some(index, carry):
        for u in range(UNROLL):
            row = index * UNROLL + u
            enter(sources, moments, slot_of(row), rows[row])
        return carry

    lax.fori_loop(0, many // UNROLL, some, 0)


def pair_sums(lists, sources, moments, leaves, records):
    blank = jnp.zeros((FEATURES, LEAF), bf16)
    rest = jnp.zeros((LEAF - FEATURES, 2 * LEAF), bf16)
    first, second = (target_features(r).astype(bf16) for r in records)
    targets = jnp.concatenate(
        [
            jnp.concatenate([first, blank], axis=1),
            rest,
            jnp.concatenate([blank, second], axis=1),
            rest,
        ],
        axis=0,
    )
    total = jnp.zeros((2 * SUMS, 2 * LEAF), f32)
    for n in range(NEIGHBOURS):
        slots = [lists[n, leaf] for leaf in leaves]
        apart = jnp.dot(
            jnp.concatenate([sources[s] for s in slots], axis=1),
            targets,
            preferred_element_type=f32,
        )
        near = jnp.maximum(apart, soften_sq)
        taper = jnp.maximum(cutoff_sq + soften_sq - near, 0.0)
        inverse = lax.rsqrt(near)
        product = taper * inverse
        weight = product * product * inverse
        high = weight.astype(bf16)
        low = (weight - high.astype(f32)).astype(bf16)
        rows = jnp.concatenate([moments[s] for s in slots], axis=0)
        total += jnp.dot(
            jnp.concatenate([rows, rows], axis=1),
            jnp.concatenate([high, low], axis=0),
            preferred_element_type=f32,
        )
    return total[:SUMS, :LEAF], total[SUMS:, LEAF:]


def moved(total, record, speed, kick):
    sums = (total[0:4] + total[4:8] + total[8:12]) * (1.0 / (cutoff_sq * cutoff_sq))
    accel = sums - record * jnp.broadcast_to(sums[3:4], sums.shape)
    row = lax.broadcasted_iota(jnp.int32, record.shape, 0)
    speed = jnp.where(row < 3, speed + time_step * (accel + kick), 0.0)
    return record + time_step * speed, speed


def group_moved(lists, sources, moments, own, speeds, kicks, leaves):
    records = [own[leaf] for leaf in leaves]
    totals = []
    for k in range(0, GROUP, 2):
        totals += pair_sums(lists, sources, moments, leaves[k : k + 2], records[k : k + 2])
    return [
        moved(total, record, speeds[leaf], kicks[leaf])
        for total, record, leaf in zip(totals, records, leaves)
    ]


def move_groups(lists, count, sources, moments, own, speeds, kicks, new_own, new_speeds, begin, end):
    def group(index, carry):
        leaves = [index * GROUP + u for u in range(GROUP)]
        results = group_moved(lists, sources, moments, own, speeds, kicks, leaves)
        for leaf, (record, speed) in zip(leaves, results):
            live = leaf < count[0]
            new_own[leaf] = jnp.where(live, record, own[leaf])
            new_speeds[leaf] = jnp.where(live, speed, speeds[leaf])
        return carry

    lax.fori_loop(begin, end, group, 0)


def choose_kernel(ids, own, chosen):
    for g in range(GHOSTS):
        chosen[g] = own[ids[g]]


def open_kernel(own, sources, moments):
    enter_all(sources, moments, own, lambda leaf: leaf, LEAVES)


def enter_ghosts(parity, sides, sources, moments):
    for q, side in enumerate(sides):
        b = jnp.where(parity[1] == 1, 2 - q, q)
        for p in range(3):
            a = jnp.where(parity[0] == 1, 2 - p, p)
            for g in range(GHOSTS):
                enter(sources, moments, LEAVES + (a * 3 + b) * GHOSTS + g, side[p * GHOSTS + g])


def ghost_kernel(
    lists, ids, parity, own, speeds, kicks, far, middle, near, old_sources, old_moments,
    sources, moments, chosen,
):
    enter_ghosts(parity, (far, middle, near), sources, moments)

    def group(index, carry):
        places = [index * GROUP + u for u in range(GROUP)]
        leaves = [ids[g] for g in places]
        results = group_moved(lists, sources, moments, own, speeds, kicks, leaves)
        for g, (record, _) in zip(places, results):
            chosen[g] = record
        return carry

    lax.fori_loop(0, GHOSTS // GROUP, group, 0)


def groups_of(count):
    return lax.div(count[0] + (GROUP - 1), GROUP)


def early_kernel(
    lists, count, own, speeds, kicks, sources, moments, new_own, new_speeds
):
    move_groups(
        lists, count, sources, moments, own, speeds, kicks, new_own, new_speeds,
        0, lax.div(groups_of(count), 2),
    )


def late_kernel(
    lists, count, own, speeds, kicks, old_sources, old_moments,
    new_own, new_speeds, sources, moments,
):
    groups = groups_of(count)
    move_groups(
        lists, count, sources, moments, own, speeds, kicks, new_own, new_speeds,
        lax.div(groups, 2), groups,
    )
    enter_all(sources, moments, new_own, lambda leaf: leaf, LEAVES)


def last_kernel(
    lists, parity, count, own, speeds, kicks, far, middle, near, old_sources, old_moments,
    new_own, new_speeds, sources, moments,
):
    enter_ghosts(parity, (far, middle, near), sources, moments)
    move_groups(
        lists, count, sources, moments, own, speeds, kicks, new_own, new_speeds,
        0, groups_of(count),
    )


VMEM = pl.BlockSpec(memory_space=pltpu.VMEM)
SMEM = pl.BlockSpec(memory_space=pltpu.SMEM)
record_shape = jax.ShapeDtypeStruct((LEAVES, 4, LEAF), f32)
chosen_shape = jax.ShapeDtypeStruct((GHOSTS, 4, LEAF), f32)
sources_shape = jax.ShapeDtypeStruct((POOL, LEAF, LEAF), bf16)
moments_shape = jax.ShapeDtypeStruct((POOL, SUMS, LEAF), bf16)


def call(kernel, name, scalars, arrays, outs, aliases=None, leaves=0):
    pairs = leaves * NEIGHBOURS * LEAF * LEAF
    return pl.pallas_call(
        kernel,
        out_shape=outs,
        in_specs=[SMEM] * len(scalars) + [VMEM] * len(arrays),
        out_specs=jax.tree.map(lambda _: VMEM, outs),
        input_output_aliases={len(scalars) + i: o for i, o in (aliases or {}).items()},
        compiler_params=pltpu.CompilerParams(vmem_limit_bytes=16 * 2**20),
        cost_estimate=pl.CostEstimate(
            flops=300 * pairs, bytes_accessed=2**20, transcendentals=pairs
        ),
        name=name,
    )(*scalars, *arrays)


def swapped(block, axis, odd):
    size = lax.axis_size(axis)
    route = []
    for i in range(odd, size + odd, 2):
        route += [(i % size, (i + 1) % size), ((i + 1) % size, i % size)]
    return lax.ppermute(block, axis, route)


def body(positions, velocities, masses, long_kick, leaf_lists, ghost_ids, leaf_counts):
    def records(parts):
        return jnp.swapaxes(parts.reshape(-1, LEAVES, LEAF), 0, 1)

    blank = jnp.zeros((1, LEAVES * LEAF), f32)
    own = records(jnp.concatenate([positions, masses[None]], axis=0))
    speeds = records(jnp.concatenate([velocities, blank], axis=0))
    kicks = records(jnp.concatenate([long_kick, blank], axis=0))
    parity = jnp.stack([lax.axis_index("gx"), lax.axis_index("gy")]).astype(jnp.int32) % 2
    lists, ids, count = leaf_lists, ghost_ids, leaf_counts

    chosen = call(choose_kernel, "choose", (ids,), (own,), chosen_shape)
    sources, moments = call(open_kernel, "open", (), (own,), (sources_shape, moments_shape))
    for subcycle in range(SUBCYCLES):
        far = swapped(chosen, "gx", 1)
        near = swapped(chosen, "gx", 0)
        if subcycle:
            own, speeds = call(
                early_kernel, "early", (lists, count), (own, speeds, kicks, sources, moments),
                (record_shape, record_shape), {0: 0, 1: 1}, LEAVES // 2,
            )
        middle = jnp.concatenate([far, chosen, near], axis=0)
        far = swapped(middle, "gy", 1)
        near = swapped(middle, "gy", 0)
        if subcycle:
            own, speeds, sources, moments = call(
                late_kernel, "late", (lists, count), (own, speeds, kicks, sources, moments),
                (record_shape, record_shape, sources_shape, moments_shape),
                {0: 0, 1: 1, 3: 2, 4: 3}, LEAVES // 2,
            )
        if subcycle < SUBCYCLES - 1:
            sources, moments, chosen = call(
                ghost_kernel, "ghost", (lists, ids, parity),
                (own, speeds, kicks, far, middle, near, sources, moments),
                (sources_shape, moments_shape, chosen_shape), {6: 0, 7: 1}, GHOSTS,
            )
        else:
            own, speeds, _, _ = call(
                last_kernel, "last", (lists, parity, count),
                (own, speeds, kicks, far, middle, near, sources, moments),
                (record_shape, record_shape, sources_shape, moments_shape),
                {0: 0, 1: 1, 6: 2, 7: 3}, LEAVES,
            )

    def whole(parts):
        return jnp.swapaxes(parts[:, :3], 0, 1).reshape(3, -1)

    return whole(own), whole(speeds)


def solution(mesh):
    split = P(("gx", "gy"))
    columns = P(None, ("gx", "gy"))
    return jax.shard_map(
        body,
        mesh=mesh,
        in_specs=(columns, columns, split, columns, columns, split, split),
        out_specs=(columns, columns),
        check_vma=False,
    )
```

```python
import jax
import jax.numpy as jnp
from jax import lax
from jax.experimental import pallas as pl
from jax.experimental.pallas import tpu as pltpu
from jax.sharding import PartitionSpec as P

SUBCYCLES = 4
LEAF = 128
LEAVES = 64
GHOSTS = 8
NEIGHBOURS = 8
POOL = LEAVES + 9 * GHOSTS
FEATURES = 32
SUMS = 16
GROUP = 8
UNROLL = 8

soften_sq = 0.04
cutoff_sq = 9.0
time_step = 0.5

f32, bf16 = jnp.float32, jnp.bfloat16


def three_parts(value):
    first = value.astype(bf16).astype(f32)
    rest = value - first
    second = rest.astype(bf16).astype(f32)
    return first, second, (rest - second).astype(bf16).astype(f32)


def norm_parts(record, more=0.0):
    square = record * record
    return three_parts(square[0:1] + square[1:2] + square[2:3] + more)


def with_row(parts, row):
    last = lax.broadcasted_iota(jnp.int32, parts.shape, 0) == 3
    return jnp.where(last, jnp.broadcast_to(row, parts.shape), parts)


def source_features(record):
    a, b, c = three_parts(record)
    n1, n2, n3 = norm_parts(record)
    one = jnp.ones_like(n1)
    zero = jnp.zeros((8, LEAF), f32)
    return jnp.concatenate(
        [
            with_row(a, n1),
            with_row(a, n2),
            with_row(b, n3),
            with_row(b, one),
            with_row(a, one),
            with_row(c, one),
            zero,
        ],
        axis=0,
    )


def target_features(record):
    a, b, c = three_parts(record * -2.0)
    n1, n2, n3 = norm_parts(record, soften_sq)
    one = jnp.ones_like(n1)
    zero = jnp.zeros((8, LEAF), f32)
    return jnp.concatenate(
        [
            with_row(a, one),
            with_row(b, one),
            with_row(a, one),
            with_row(b, n1),
            with_row(c, n2),
            with_row(a, n3),
            zero,
        ],
        axis=0,
    )


def moment_rows(record):
    mass = jnp.broadcast_to(record[3:4], record.shape)
    a, b, c = three_parts(with_row(record, jnp.ones((1, LEAF), f32)) * mass)
    return jnp.concatenate([a, b, c, jnp.zeros_like(a)], axis=0).astype(bf16)


def enter(sources, moments, slot, record):
    features = source_features(record)
    blank = jnp.zeros((LEAF - FEATURES, LEAF), f32)
    sources[slot] = jnp.concatenate([features, blank], axis=0).T.astype(bf16)
    moments[slot] = moment_rows(record)


def enter_all(sources, moments, rows, slot_of, many):
    def some(index, carry):
        for u in range(UNROLL):
            row = index * UNROLL + u
            enter(sources, moments, slot_of(row), rows[row])
        return carry

    lax.fori_loop(0, many // UNROLL, some, 0)


def pair_sums(lists, sources, moments, leaves, records):
    blank = jnp.zeros((FEATURES, LEAF), bf16)
    rest = jnp.zeros((LEAF - FEATURES, 2 * LEAF), bf16)
    first, second = (target_features(r).astype(bf16) for r in records)
    targets = jnp.concatenate(
        [
            jnp.concatenate([first, blank], axis=1),
            rest,
            jnp.concatenate([blank, second], axis=1),
            rest,
        ],
        axis=0,
    )
    slots = [[lists[n, leaf] for leaf in leaves] for n in range(NEIGHBOURS)]
    apart = jnp.dot(
        jnp.concatenate([jnp.concatenate([sources[s] for s in pair], axis=1) for pair in slots], axis=0),
        targets,
        preferred_element_type=f32,
    )
    weights, rows = [], []
    for n, pair in enumerate(slots):
        near = jnp.maximum(apart[n * LEAF : (n + 1) * LEAF], soften_sq)
        taper = jnp.maximum(cutoff_sq + soften_sq - near, 0.0)
        inverse = lax.rsqrt(near)
        product = taper * inverse
        weight = product * product * inverse
        high = weight.astype(bf16)
        low = (weight - high.astype(f32)).astype(bf16)
        weights += [high, low]
        rows += [jnp.concatenate([moments[s] for s in pair], axis=0)] * 2
    total = jnp.dot(
        jnp.concatenate(rows, axis=1),
        jnp.concatenate(weights, axis=0),
        preferred_element_type=f32,
    )
    return total[:SUMS, :LEAF], total[SUMS:, LEAF:]


def moved(total, record, speed, kick):
    sums = (total[0:4] + total[4:8] + total[8:12]) * (1.0 / (cutoff_sq * cutoff_sq))
    accel = sums - record * jnp.broadcast_to(sums[3:4], sums.shape)
    row = lax.broadcasted_iota(jnp.int32, record.shape, 0)
    speed = jnp.where(row < 3, speed + time_step * (accel + kick), 0.0)
    return record + time_step * speed, speed


def group_moved(lists, sources, moments, own, speeds, kicks, leaves):
    records = [own[leaf] for leaf in leaves]
    totals = []
    for k in range(0, GROUP, 2):
        totals += pair_sums(lists, sources, moments, leaves[k : k + 2], records[k : k + 2])
    return [
        moved(total, record, speeds[leaf], kicks[leaf])
        for total, record, leaf in zip(totals, records, leaves)
    ]


def move_groups(lists, count, sources, moments, own, speeds, kicks, new_own, new_speeds, begin, end):
    def group(index, carry):
        leaves = [index * GROUP + u for u in range(GROUP)]
        results = group_moved(lists, sources, moments, own, speeds, kicks, leaves)
        for leaf, (record, speed) in zip(leaves, results):
            live = leaf < count[0]
            new_own[leaf] = jnp.where(live, record, own[leaf])
            new_speeds[leaf] = jnp.where(live, speed, speeds[leaf])
        return carry

    lax.fori_loop(begin, end, group, 0)


def lanes(leaf):
    return pl.ds(pl.multiple_of(leaf * LEAF, LEAF), LEAF)


def first_record(positions, masses, leaf):
    return jnp.concatenate([positions[:, lanes(leaf)], masses[:, lanes(leaf)]], axis=0)


def choose_kernel(ids, positions, masses, chosen):
    for g in range(GHOSTS):
        chosen[g] = first_record(positions, masses, ids[g])


def open_kernel(positions, velocities, masses, long_kick, own, speeds, kicks, sources, moments):
    blank = jnp.zeros((1, LEAF), f32)

    def some(index, carry):
        for u in range(UNROLL):
            leaf = index * UNROLL + u
            record = first_record(positions, masses, leaf)
            own[leaf] = record
            speeds[leaf] = jnp.concatenate([velocities[:, lanes(leaf)], blank], axis=0)
            kicks[leaf] = jnp.concatenate([long_kick[:, lanes(leaf)], blank], axis=0)
            enter(sources, moments, leaf, record)
        return carry

    lax.fori_loop(0, LEAVES // UNROLL, some, 0)


def enter_ghosts(parity, sides, sources, moments):
    for q, side in enumerate(sides):
        b = jnp.where(parity[1] == 1, 2 - q, q)
        for p in range(3):
            a = jnp.where(parity[0] == 1, 2 - p, p)
            for g in range(GHOSTS):
                enter(sources, moments, LEAVES + (a * 3 + b) * GHOSTS + g, side[p * GHOSTS + g])


def ghost_kernel(
    lists, ids, parity, own, speeds, kicks, far, middle, near, old_sources, old_moments,
    sources, moments, chosen,
):
    enter_ghosts(parity, (far, middle, near), sources, moments)

    results = group_moved(
        lists, sources, moments, own, speeds, kicks, [ids[g] for g in range(GHOSTS)]
    )
    for g, (record, _) in enumerate(results):
        chosen[g] = record


def groups_of(count):
    return lax.div(count[0] + (GROUP - 1), GROUP)


def early_kernel(
    lists, count, own, speeds, kicks, sources, moments, new_own, new_speeds
):
    move_groups(
        lists, count, sources, moments, own, speeds, kicks, new_own, new_speeds,
        0, lax.div(groups_of(count), 2),
    )


def late_kernel(
    lists, count, own, speeds, kicks, old_sources, old_moments,
    new_own, new_speeds, sources, moments,
):
    groups = groups_of(count)
    move_groups(
        lists, count, sources, moments, own, speeds, kicks, new_own, new_speeds,
        lax.div(groups, 2), groups,
    )
    enter_all(sources, moments, new_own, lambda leaf: leaf, LEAVES)


def last_kernel(
    lists, parity, count, own, speeds, kicks, far, middle, near, old_sources, old_moments,
    places, paces, sources, moments,
):
    enter_ghosts(parity, (far, middle, near), sources, moments)

    def group(index, carry):
        leaves = [index * GROUP + u for u in range(GROUP)]
        results = group_moved(lists, sources, moments, own, speeds, kicks, leaves)
        for leaf, (record, speed) in zip(leaves, results):
            live = leaf < count[0]
            places[:, lanes(leaf)] = jnp.where(live, record, own[leaf])[:3]
            paces[:, lanes(leaf)] = jnp.where(live, speed, speeds[leaf])[:3]
        return carry

    def keep(leaf, carry):
        places[:, lanes(leaf)] = own[leaf][:3]
        paces[:, lanes(leaf)] = speeds[leaf][:3]
        return carry

    groups = groups_of(count)
    lax.fori_loop(0, groups, group, 0)
    lax.fori_loop(groups * GROUP, LEAVES, keep, 0)


VMEM = pl.BlockSpec(memory_space=pltpu.VMEM)
SMEM = pl.BlockSpec(memory_space=pltpu.SMEM)
record_shape = jax.ShapeDtypeStruct((LEAVES, 4, LEAF), f32)
whole_shape = jax.ShapeDtypeStruct((3, LEAVES * LEAF), f32)
chosen_shape = jax.ShapeDtypeStruct((GHOSTS, 4, LEAF), f32)
sources_shape = jax.ShapeDtypeStruct((POOL, LEAF, LEAF), bf16)
moments_shape = jax.ShapeDtypeStruct((POOL, SUMS, LEAF), bf16)


def call(kernel, name, scalars, arrays, outs, aliases=None, leaves=0):
    pairs = leaves * NEIGHBOURS * LEAF * LEAF
    return pl.pallas_call(
        kernel,
        out_shape=outs,
        in_specs=[SMEM] * len(scalars) + [VMEM] * len(arrays),
        out_specs=jax.tree.map(lambda _: VMEM, outs),
        input_output_aliases={len(scalars) + i: o for i, o in (aliases or {}).items()},
        compiler_params=pltpu.CompilerParams(vmem_limit_bytes=16 * 2**20),
        cost_estimate=pl.CostEstimate(
            flops=300 * pairs, bytes_accessed=2**20, transcendentals=pairs
        ),
        name=name,
    )(*scalars, *arrays)


def swapped(block, axis, odd):
    size = lax.axis_size(axis)
    route = []
    for i in range(odd, size + odd, 2):
        route += [(i % size, (i + 1) % size), ((i + 1) % size, i % size)]
    return lax.ppermute(block, axis, route)


def body(positions, velocities, masses, long_kick, leaf_lists, ghost_ids, leaf_counts):
    parity = jnp.stack([lax.axis_index("gx"), lax.axis_index("gy")]).astype(jnp.int32) % 2
    lists, ids, count = leaf_lists, ghost_ids, leaf_counts

    masses = masses[None]
    chosen = call(choose_kernel, "choose", (ids,), (positions, masses), chosen_shape)
    own, speeds, kicks, sources, moments = call(
        open_kernel, "open", (), (positions, velocities, masses, long_kick),
        (record_shape,) * 3 + (sources_shape, moments_shape),
    )
    for subcycle in range(SUBCYCLES):
        far = swapped(chosen, "gx", 1)
        near = swapped(chosen, "gx", 0)
        if subcycle:
            own, speeds = call(
                early_kernel, "early", (lists, count), (own, speeds, kicks, sources, moments),
                (record_shape, record_shape), {0: 0, 1: 1}, LEAVES // 2,
            )
        middle = jnp.concatenate([far, chosen, near], axis=0)
        far = swapped(middle, "gy", 1)
        near = swapped(middle, "gy", 0)
        if subcycle:
            own, speeds, sources, moments = call(
                late_kernel, "late", (lists, count), (own, speeds, kicks, sources, moments),
                (record_shape, record_shape, sources_shape, moments_shape),
                {0: 0, 1: 1, 3: 2, 4: 3}, LEAVES // 2,
            )
        if subcycle < SUBCYCLES - 1:
            sources, moments, chosen = call(
                ghost_kernel, "ghost", (lists, ids, parity),
                (own, speeds, kicks, far, middle, near, sources, moments),
                (sources_shape, moments_shape, chosen_shape), {6: 0, 7: 1}, GHOSTS,
            )
        else:
            places, paces, _, _ = call(
                last_kernel, "last", (lists, parity, count),
                (own, speeds, kicks, far, middle, near, sources, moments),
                (whole_shape, whole_shape, sources_shape, moments_shape),
                {6: 2, 7: 3}, LEAVES,
            )
    return places, paces


def solution(mesh):
    split = P(("gx", "gy"))
    columns = P(None, ("gx", "gy"))
    return jax.shard_map(
        body,
        mesh=mesh,
        in_specs=(columns, columns, split, columns, columns, split, split),
        out_specs=(columns, columns),
        check_vma=False,
    )
```

```python
import jax
import jax.numpy as jnp
from jax import lax
from jax.experimental import pallas as pl
from jax.experimental.pallas import tpu as pltpu
from jax.sharding import PartitionSpec as P

SUBCYCLES = 4
LEAF = 128
LEAVES = 64
GHOSTS = 8
NEIGHBOURS = 8
POOL = LEAVES + 9 * GHOSTS
FEATURES = 32
SUMS = 16
GROUP = 8
UNROLL = 8

soften_sq = 0.04
cutoff_sq = 9.0
time_step = 0.5

f32, bf16 = jnp.float32, jnp.bfloat16


def three_parts(value):
    first = value.astype(bf16).astype(f32)
    rest = value - first
    second = rest.astype(bf16).astype(f32)
    return first, second, (rest - second).astype(bf16).astype(f32)


def norm_parts(record, more=0.0):
    square = record * record
    return three_parts(square[0:1] + square[1:2] + square[2:3] + more)


def with_row(parts, row):
    last = lax.broadcasted_iota(jnp.int32, parts.shape, 0) == 3
    return jnp.where(last, jnp.broadcast_to(row, parts.shape), parts)


def source_features(record):
    a, b, c = three_parts(record)
    n1, n2, n3 = norm_parts(record)
    one = jnp.ones_like(n1)
    zero = jnp.zeros((8, LEAF), f32)
    return jnp.concatenate(
        [
            with_row(a, n1),
            with_row(a, n2),
            with_row(b, n3),
            with_row(b, one),
            with_row(a, one),
            with_row(c, one),
            zero,
        ],
        axis=0,
    )


def target_features(record):
    a, b, c = three_parts(record * -2.0)
    n1, n2, n3 = norm_parts(record, soften_sq)
    one = jnp.ones_like(n1)
    zero = jnp.zeros((8, LEAF), f32)
    return jnp.concatenate(
        [
            with_row(a, one),
            with_row(b, one),
            with_row(a, one),
            with_row(b, n1),
            with_row(c, n2),
            with_row(a, n3),
            zero,
        ],
        axis=0,
    )


def moment_rows(record):
    mass = jnp.broadcast_to(record[3:4], record.shape)
    a, b, c = three_parts(with_row(record, jnp.ones((1, LEAF), f32)) * mass)
    return jnp.concatenate([a, b, c, jnp.zeros_like(a)], axis=0).astype(bf16)


def enter(sources, moments, slot, record):
    features = source_features(record)
    blank = jnp.zeros((LEAF - FEATURES, LEAF), f32)
    sources[slot] = jnp.concatenate([features, blank], axis=0).T.astype(bf16)
    moments[slot] = moment_rows(record)


def enter_all(sources, moments, rows, slot_of, many):
    def some(index, carry):
        for u in range(UNROLL):
            row = index * UNROLL + u
            enter(sources, moments, slot_of(row), rows[row])
        return carry

    lax.fori_loop(0, many // UNROLL, some, 0)


def pair_sums(lists, sources, moments, leaves, records):
    blank = jnp.zeros((FEATURES, LEAF), bf16)
    rest = jnp.zeros((LEAF - FEATURES, 2 * LEAF), bf16)
    first, second = (target_features(r).astype(bf16) for r in records)
    targets = jnp.concatenate(
        [
            jnp.concatenate([first, blank], axis=1),
            rest,
            jnp.concatenate([blank, second], axis=1),
            rest,
        ],
        axis=0,
    )
    slots = [[lists[n, leaf] for leaf in leaves] for n in range(NEIGHBOURS)]
    apart = jnp.dot(
        jnp.concatenate([jnp.concatenate([sources[s] for s in pair], axis=1) for pair in slots], axis=0),
        targets,
        preferred_element_type=f32,
    )
    weights, rows = [], []
    for n, pair in enumerate(slots):
        near = jnp.maximum(apart[n * LEAF : (n + 1) * LEAF], soften_sq)
        taper = jnp.maximum(cutoff_sq + soften_sq - near, 0.0)
        inverse = lax.rsqrt(near)
        product = taper * inverse
        weight = product * product * inverse
        high = weight.astype(bf16)
        low = (weight - high.astype(f32)).astype(bf16)
        weights += [high, low]
        rows += [jnp.concatenate([moments[s] for s in pair], axis=0)] * 2
    total = jnp.dot(
        jnp.concatenate(rows, axis=1),
        jnp.concatenate(weights, axis=0),
        preferred_element_type=f32,
    )
    return total[:SUMS, :LEAF], total[SUMS:, LEAF:]


def moved(total, record, speed, kick):
    sums = (total[0:4] + total[4:8] + total[8:12]) * (1.0 / (cutoff_sq * cutoff_sq))
    accel = sums - record * jnp.broadcast_to(sums[3:4], sums.shape)
    row = lax.broadcasted_iota(jnp.int32, record.shape, 0)
    speed = jnp.where(row < 3, speed + time_step * (accel + kick), 0.0)
    return record + time_step * speed, speed


def group_moved(lists, sources, moments, own, speeds, kicks, leaves):
    records = [own[leaf] for leaf in leaves]
    totals = []
    for k in range(0, GROUP, 2):
        totals += pair_sums(lists, sources, moments, leaves[k : k + 2], records[k : k + 2])
    return [
        moved(total, record, speeds[leaf], kicks[leaf])
        for total, record, leaf in zip(totals, records, leaves)
    ]


def move_groups(lists, count, sources, moments, own, speeds, kicks, new_own, new_speeds, begin, end):
    def group(index, carry):
        leaves = [index * GROUP + u for u in range(GROUP)]
        results = group_moved(lists, sources, moments, own, speeds, kicks, leaves)
        for leaf, (record, speed) in zip(leaves, results):
            live = leaf < count[0]
            new_own[leaf] = jnp.where(live, record, own[leaf])
            new_speeds[leaf] = jnp.where(live, speed, speeds[leaf])
        return carry

    lax.fori_loop(begin, end, group, 0)


def lanes(leaf):
    return pl.ds(pl.multiple_of(leaf * LEAF, LEAF), LEAF)


def first_record(positions, masses, leaf):
    return jnp.concatenate([positions[:, lanes(leaf)], masses[:, lanes(leaf)]], axis=0)


def choose_kernel(ids, positions, masses, chosen):
    for g in range(GHOSTS):
        chosen[g] = first_record(positions, masses, ids[g])


def open_kernel(positions, velocities, masses, long_kick, own, speeds, kicks, sources, moments):
    blank = jnp.zeros((1, LEAF), f32)

    def some(index, carry):
        for u in range(UNROLL):
            leaf = index * UNROLL + u
            record = first_record(positions, masses, leaf)
            own[leaf] = record
            speeds[leaf] = jnp.concatenate([velocities[:, lanes(leaf)], blank], axis=0)
            kicks[leaf] = jnp.concatenate([long_kick[:, lanes(leaf)], blank], axis=0)
            enter(sources, moments, leaf, record)
        return carry

    lax.fori_loop(0, LEAVES // UNROLL, some, 0)


def enter_ghosts(parity, sides, sources, moments):
    for q, side in sides.items():
        b = jnp.where(parity[1] == 1, q, 2 - q)
        for p in range(3):
            a = jnp.where(parity[0] == 1, p, 2 - p)
            for g in range(GHOSTS):
                enter(sources, moments, LEAVES + (a * 3 + b) * GHOSTS + g, side[p * GHOSTS + g])


def ghost_kernel(
    lists, ids, parity, own, speeds, kicks, near, far, old_sources, old_moments,
    sources, moments, chosen,
):
    enter_ghosts(parity, {0: near, 2: far}, sources, moments)

    results = group_moved(
        lists, sources, moments, own, speeds, kicks, [ids[g] for g in range(GHOSTS)]
    )
    for g, (record, _) in enumerate(results):
        chosen[g] = record


def groups_of(count):
    return lax.div(count[0] + (GROUP - 1), GROUP)


def early_kernel(
    lists, count, own, speeds, kicks, sources, moments, new_own, new_speeds
):
    move_groups(
        lists, count, sources, moments, own, speeds, kicks, new_own, new_speeds,
        0, lax.div(groups_of(count), 2),
    )


def middle_kernel(parity, middle, old_sources, old_moments, sources, moments):
    enter_ghosts(parity, {1: middle}, sources, moments)


def late_kernel(
    lists, parity, count, own, speeds, kicks, middle, old_sources, old_moments,
    new_own, new_speeds, sources, moments,
):
    groups = groups_of(count)
    move_groups(
        lists, count, sources, moments, own, speeds, kicks, new_own, new_speeds,
        lax.div(groups, 2), groups,
    )
    enter_all(sources, moments, new_own, lambda leaf: leaf, LEAVES)
    enter_ghosts(parity, {1: middle}, sources, moments)


def last_kernel(
    lists, parity, count, own, speeds, kicks, near, far, old_sources, old_moments,
    places, paces, sources, moments,
):
    enter_ghosts(parity, {0: near, 2: far}, sources, moments)

    def group(index, carry):
        leaves = [index * GROUP + u for u in range(GROUP)]
        results = group_moved(lists, sources, moments, own, speeds, kicks, leaves)
        for leaf, (record, speed) in zip(leaves, results):
            live = leaf < count[0]
            places[:, lanes(leaf)] = jnp.where(live, record, own[leaf])[:3]
            paces[:, lanes(leaf)] = jnp.where(live, speed, speeds[leaf])[:3]
        return carry

    def keep(leaf, carry):
        places[:, lanes(leaf)] = own[leaf][:3]
        paces[:, lanes(leaf)] = speeds[leaf][:3]
        return carry

    groups = groups_of(count)
    lax.fori_loop(0, groups, group, 0)
    lax.fori_loop(groups * GROUP, LEAVES, keep, 0)


VMEM = pl.BlockSpec(memory_space=pltpu.VMEM)
SMEM = pl.BlockSpec(memory_space=pltpu.SMEM)
record_shape = jax.ShapeDtypeStruct((LEAVES, 4, LEAF), f32)
whole_shape = jax.ShapeDtypeStruct((3, LEAVES * LEAF), f32)
chosen_shape = jax.ShapeDtypeStruct((GHOSTS, 4, LEAF), f32)
sources_shape = jax.ShapeDtypeStruct((POOL, LEAF, LEAF), bf16)
moments_shape = jax.ShapeDtypeStruct((POOL, SUMS, LEAF), bf16)


def call(kernel, name, scalars, arrays, outs, aliases=None, leaves=0):
    pairs = leaves * NEIGHBOURS * LEAF * LEAF
    return pl.pallas_call(
        kernel,
        out_shape=outs,
        in_specs=[SMEM] * len(scalars) + [VMEM] * len(arrays),
        out_specs=jax.tree.map(lambda _: VMEM, outs),
        input_output_aliases={len(scalars) + i: o for i, o in (aliases or {}).items()},
        compiler_params=pltpu.CompilerParams(vmem_limit_bytes=16 * 2**20),
        cost_estimate=pl.CostEstimate(
            flops=300 * pairs, bytes_accessed=2**20, transcendentals=pairs
        ),
        name=name,
    )(*scalars, *arrays)


def swapped(block, axis, odd):
    size = lax.axis_size(axis)
    route = []
    for i in range(odd, size + odd, 2):
        route += [(i % size, (i + 1) % size), ((i + 1) % size, i % size)]
    return lax.ppermute(block, axis, route)


def body(positions, velocities, masses, long_kick, leaf_lists, ghost_ids, leaf_counts):
    parity = jnp.stack([lax.axis_index("gx"), lax.axis_index("gy")]).astype(jnp.int32) % 2
    lists, ids, count = leaf_lists, ghost_ids, leaf_counts

    masses = masses[None]
    chosen = call(choose_kernel, "choose", (ids,), (positions, masses), chosen_shape)
    own, speeds, kicks, sources, moments = call(
        open_kernel, "open", (), (positions, velocities, masses, long_kick),
        (record_shape,) * 3 + (sources_shape, moments_shape),
    )
    for subcycle in range(SUBCYCLES):
        far = swapped(chosen, "gx", 1)
        near = swapped(chosen, "gx", 0)
        if subcycle:
            own, speeds = call(
                early_kernel, "early", (lists, count), (own, speeds, kicks, sources, moments),
                (record_shape, record_shape), {0: 0, 1: 1}, LEAVES // 2,
            )
        middle = jnp.concatenate([near, chosen, far], axis=0)
        if not subcycle:
            middle, own = lax.optimization_barrier((middle, own))
        far = swapped(middle, "gy", 1)
        near = swapped(middle, "gy", 0)
        if subcycle:
            own, speeds, sources, moments = call(
                late_kernel, "late", (lists, parity, count),
                (own, speeds, kicks, middle, sources, moments),
                (record_shape, record_shape, sources_shape, moments_shape),
                {0: 0, 1: 1, 4: 2, 5: 3}, LEAVES // 2,
            )
        else:
            sources, moments = call(
                middle_kernel, "middle", (parity,), (middle, sources, moments),
                (sources_shape, moments_shape), {1: 0, 2: 1}, 1,
            )
        if subcycle < SUBCYCLES - 1:
            sources, moments, chosen = call(
                ghost_kernel, "ghost", (lists, ids, parity),
                (own, speeds, kicks, near, far, sources, moments),
                (sources_shape, moments_shape, chosen_shape), {5: 0, 6: 1}, GHOSTS,
            )
        else:
            places, paces, _, _ = call(
                last_kernel, "last", (lists, parity, count),
                (own, speeds, kicks, near, far, sources, moments),
                (whole_shape, whole_shape, sources_shape, moments_shape),
                {5: 2, 6: 3}, LEAVES,
            )
    return places, paces


def solution(mesh):
    split = P(("gx", "gy"))
    columns = P(None, ("gx", "gy"))
    return jax.shard_map(
        body,
        mesh=mesh,
        in_specs=(columns, columns, split, columns, columns, split, split),
        out_specs=(columns, columns),
        check_vma=False,
    )
```

```python
import jax
import jax.numpy as jnp
from jax import lax
from jax.experimental import pallas as pl
from jax.experimental.pallas import tpu as pltpu
from jax.sharding import PartitionSpec as P

SUBCYCLES = 4
LEAF = 128
LEAVES = 64
GHOSTS = 8
NEIGHBOURS = 8
POOL = LEAVES + 9 * GHOSTS
FEATURES = 32
SUMS = 16
GROUP = 16
UNROLL = 8

soften_sq = 0.04
cutoff_sq = 9.0
time_step = 0.5

f32, bf16 = jnp.float32, jnp.bfloat16


def three_parts(value):
    first = value.astype(bf16).astype(f32)
    rest = value - first
    second = rest.astype(bf16).astype(f32)
    return first, second, (rest - second).astype(bf16).astype(f32)


def norm_parts(record, more=0.0):
    square = record * record
    return three_parts(square[0:1] + square[1:2] + square[2:3] + more)


def with_row(parts, row):
    last = lax.broadcasted_iota(jnp.int32, parts.shape, 0) == 3
    return jnp.where(last, jnp.broadcast_to(row, parts.shape), parts)


def source_features(record):
    a, b, c = three_parts(record)
    n1, n2, n3 = norm_parts(record)
    one = jnp.ones_like(n1)
    zero = jnp.zeros((8, LEAF), f32)
    return jnp.concatenate(
        [
            with_row(a, n1),
            with_row(a, n2),
            with_row(b, n3),
            with_row(b, one),
            with_row(a, one),
            with_row(c, one),
            zero,
        ],
        axis=0,
    )


def target_features(record):
    a, b, c = three_parts(record * -2.0)
    n1, n2, n3 = norm_parts(record, soften_sq)
    one = jnp.ones_like(n1)
    zero = jnp.zeros((8, LEAF), f32)
    return jnp.concatenate(
        [
            with_row(a, one),
            with_row(b, one),
            with_row(a, one),
            with_row(b, n1),
            with_row(c, n2),
            with_row(a, n3),
            zero,
        ],
        axis=0,
    )


def moment_rows(record):
    mass = jnp.broadcast_to(record[3:4], record.shape)
    a, b, c = three_parts(with_row(record, jnp.ones((1, LEAF), f32)) * mass)
    return jnp.concatenate([a, b, c, jnp.zeros_like(a)], axis=0).astype(bf16)


def enter(sources, moments, slot, record):
    features = source_features(record)
    blank = jnp.zeros((LEAF - FEATURES, LEAF), f32)
    sources[slot] = jnp.concatenate([features, blank], axis=0).T.astype(bf16)
    moments[slot] = moment_rows(record)


def enter_all(sources, moments, rows, slot_of, many):
    def some(index, carry):
        for u in range(UNROLL):
            row = index * UNROLL + u
            enter(sources, moments, slot_of(row), rows[row])
        return carry

    lax.fori_loop(0, many // UNROLL, some, 0)


def pair_sums(lists, sources, moments, leaves, records):
    blank = jnp.zeros((FEATURES, LEAF), bf16)
    rest = jnp.zeros((LEAF - FEATURES, 2 * LEAF), bf16)
    first, second = (target_features(r).astype(bf16) for r in records)
    targets = jnp.concatenate(
        [
            jnp.concatenate([first, blank], axis=1),
            rest,
            jnp.concatenate([blank, second], axis=1),
            rest,
        ],
        axis=0,
    )
    slots = [[lists[n, leaf] for leaf in leaves] for n in range(NEIGHBOURS)]
    apart = jnp.dot(
        jnp.concatenate([jnp.concatenate([sources[s] for s in pair], axis=1) for pair in slots], axis=0),
        targets,
        preferred_element_type=f32,
    )
    weights, rows = [], []
    for n, pair in enumerate(slots):
        near = jnp.maximum(apart[n * LEAF : (n + 1) * LEAF], soften_sq)
        taper = jnp.maximum(cutoff_sq + soften_sq - near, 0.0)
        inverse = lax.rsqrt(near)
        product = taper * inverse
        weight = product * product * inverse
        high = weight.astype(bf16)
        low = (weight - high.astype(f32)).astype(bf16)
        weights += [high, low]
        rows += [jnp.concatenate([moments[s] for s in pair], axis=0)] * 2
    total = jnp.dot(
        jnp.concatenate(rows, axis=1),
        jnp.concatenate(weights, axis=0),
        preferred_element_type=f32,
    )
    return total[:SUMS, :LEAF], total[SUMS:, LEAF:]


def moved(total, record, speed, kick):
    sums = (total[0:4] + total[4:8] + total[8:12]) * (1.0 / (cutoff_sq * cutoff_sq))
    accel = sums - record * jnp.broadcast_to(sums[3:4], sums.shape)
    row = lax.broadcasted_iota(jnp.int32, record.shape, 0)
    speed = jnp.where(row < 3, speed + time_step * (accel + kick), 0.0)
    return record + time_step * speed, speed


def group_moved(lists, sources, moments, own, speeds, kicks, leaves):
    records = [own[leaf] for leaf in leaves]
    totals = []
    for k in range(0, len(leaves), 2):
        totals += pair_sums(lists, sources, moments, leaves[k : k + 2], records[k : k + 2])
    return [
        moved(total, record, speeds[leaf], kicks[leaf])
        for total, record, leaf in zip(totals, records, leaves)
    ]


def move_groups(lists, count, sources, moments, own, speeds, kicks, new_own, new_speeds, begin, end):
    def group(index, carry):
        leaves = [index * GROUP + u for u in range(GROUP)]
        results = group_moved(lists, sources, moments, own, speeds, kicks, leaves)
        for leaf, (record, speed) in zip(leaves, results):
            live = leaf < count[0]
            new_own[leaf] = jnp.where(live, record, own[leaf])
            new_speeds[leaf] = jnp.where(live, speed, speeds[leaf])
        return carry

    lax.fori_loop(begin, end, group, 0)


def lanes(leaf):
    return pl.ds(pl.multiple_of(leaf * LEAF, LEAF), LEAF)


def first_record(positions, masses, leaf):
    return jnp.concatenate([positions[:, lanes(leaf)], masses[:, lanes(leaf)]], axis=0)


def choose_kernel(ids, positions, masses, chosen):
    for g in range(GHOSTS):
        chosen[g] = first_record(positions, masses, ids[g])


def open_kernel(positions, velocities, masses, long_kick, own, speeds, kicks, sources, moments):
    blank = jnp.zeros((1, LEAF), f32)

    def some(index, carry):
        for u in range(UNROLL):
            leaf = index * UNROLL + u
            record = first_record(positions, masses, leaf)
            own[leaf] = record
            speeds[leaf] = jnp.concatenate([velocities[:, lanes(leaf)], blank], axis=0)
            kicks[leaf] = jnp.concatenate([long_kick[:, lanes(leaf)], blank], axis=0)
            enter(sources, moments, leaf, record)
        return carry

    lax.fori_loop(0, LEAVES // UNROLL, some, 0)


def enter_ghosts(parity, sides, sources, moments):
    for q, side in sides.items():
        b = jnp.where(parity[1] == 1, q, 2 - q)
        for p in range(3):
            a = jnp.where(parity[0] == 1, p, 2 - p)
            for g in range(GHOSTS):
                enter(sources, moments, LEAVES + (a * 3 + b) * GHOSTS + g, side[p * GHOSTS + g])


def ghost_kernel(
    lists, ids, parity, own, speeds, kicks, near, far, old_sources, old_moments,
    sources, moments, chosen,
):
    enter_ghosts(parity, {0: near, 2: far}, sources, moments)

    results = group_moved(
        lists, sources, moments, own, speeds, kicks, [ids[g] for g in range(GHOSTS)]
    )
    for g, (record, _) in enumerate(results):
        chosen[g] = record


def groups_of(count):
    return lax.div(count[0] + (GROUP - 1), GROUP)


def early_kernel(
    lists, count, own, speeds, kicks, sources, moments, new_own, new_speeds
):
    move_groups(
        lists, count, sources, moments, own, speeds, kicks, new_own, new_speeds,
        0, lax.div(groups_of(count), 2),
    )


def middle_kernel(parity, middle, old_sources, old_moments, sources, moments):
    enter_ghosts(parity, {1: middle}, sources, moments)


def late_kernel(
    lists, parity, count, own, speeds, kicks, middle, old_sources, old_moments,
    new_own, new_speeds, sources, moments,
):
    groups = groups_of(count)
    move_groups(
        lists, count, sources, moments, own, speeds, kicks, new_own, new_speeds,
        lax.div(groups, 2), groups,
    )
    enter_all(sources, moments, new_own, lambda leaf: leaf, LEAVES)
    enter_ghosts(parity, {1: middle}, sources, moments)


def last_kernel(
    lists, parity, count, own, speeds, kicks, near, far, old_sources, old_moments,
    places, paces, sources, moments,
):
    enter_ghosts(parity, {0: near, 2: far}, sources, moments)

    def group(index, carry):
        leaves = [index * GROUP + u for u in range(GROUP)]
        results = group_moved(lists, sources, moments, own, speeds, kicks, leaves)
        for leaf, (record, speed) in zip(leaves, results):
            live = leaf < count[0]
            places[:, lanes(leaf)] = jnp.where(live, record, own[leaf])[:3]
            paces[:, lanes(leaf)] = jnp.where(live, speed, speeds[leaf])[:3]
        return carry

    def keep(leaf, carry):
        places[:, lanes(leaf)] = own[leaf][:3]
        paces[:, lanes(leaf)] = speeds[leaf][:3]
        return carry

    groups = groups_of(count)
    lax.fori_loop(0, groups, group, 0)
    lax.fori_loop(groups * GROUP, LEAVES, keep, 0)


VMEM = pl.BlockSpec(memory_space=pltpu.VMEM)
SMEM = pl.BlockSpec(memory_space=pltpu.SMEM)
record_shape = jax.ShapeDtypeStruct((LEAVES, 4, LEAF), f32)
whole_shape = jax.ShapeDtypeStruct((3, LEAVES * LEAF), f32)
chosen_shape = jax.ShapeDtypeStruct((GHOSTS, 4, LEAF), f32)
sources_shape = jax.ShapeDtypeStruct((POOL, LEAF, LEAF), bf16)
moments_shape = jax.ShapeDtypeStruct((POOL, SUMS, LEAF), bf16)


def call(kernel, name, scalars, arrays, outs, aliases=None, leaves=0):
    pairs = leaves * NEIGHBOURS * LEAF * LEAF
    return pl.pallas_call(
        kernel,
        out_shape=outs,
        in_specs=[SMEM] * len(scalars) + [VMEM] * len(arrays),
        out_specs=jax.tree.map(lambda _: VMEM, outs),
        input_output_aliases={len(scalars) + i: o for i, o in (aliases or {}).items()},
        compiler_params=pltpu.CompilerParams(vmem_limit_bytes=16 * 2**20),
        cost_estimate=pl.CostEstimate(
            flops=300 * pairs, bytes_accessed=2**20, transcendentals=pairs
        ),
        name=name,
    )(*scalars, *arrays)


def swapped(block, axis, odd):
    size = lax.axis_size(axis)
    route = []
    for i in range(odd, size + odd, 2):
        route += [(i % size, (i + 1) % size), ((i + 1) % size, i % size)]
    return lax.ppermute(block, axis, route)


def body(positions, velocities, masses, long_kick, leaf_lists, ghost_ids, leaf_counts):
    parity = jnp.stack([lax.axis_index("gx"), lax.axis_index("gy")]).astype(jnp.int32) % 2
    lists, ids, count = leaf_lists, ghost_ids, leaf_counts

    masses = masses[None]
    chosen = call(choose_kernel, "choose", (ids,), (positions, masses), chosen_shape)
    own, speeds, kicks, sources, moments = call(
        open_kernel, "open", (), (positions, velocities, masses, long_kick),
        (record_shape,) * 3 + (sources_shape, moments_shape),
    )
    for subcycle in range(SUBCYCLES):
        far = swapped(chosen, "gx", 1)
        near = swapped(chosen, "gx", 0)
        if subcycle:
            own, speeds = call(
                early_kernel, "early", (lists, count), (own, speeds, kicks, sources, moments),
                (record_shape, record_shape), {0: 0, 1: 1}, LEAVES // 2,
            )
        middle = jnp.concatenate([near, chosen, far], axis=0)
        if not subcycle:
            middle, own = lax.optimization_barrier((middle, own))
        far = swapped(middle, "gy", 1)
        near = swapped(middle, "gy", 0)
        if subcycle:
            own, speeds, sources, moments = call(
                late_kernel, "late", (lists, parity, count),
                (own, speeds, kicks, middle, sources, moments),
                (record_shape, record_shape, sources_shape, moments_shape),
                {0: 0, 1: 1, 4: 2, 5: 3}, LEAVES // 2,
            )
        else:
            sources, moments = call(
                middle_kernel, "middle", (parity,), (middle, sources, moments),
                (sources_shape, moments_shape), {1: 0, 2: 1}, 1,
            )
        if subcycle < SUBCYCLES - 1:
            sources, moments, chosen = call(
                ghost_kernel, "ghost", (lists, ids, parity),
                (own, speeds, kicks, near, far, sources, moments),
                (sources_shape, moments_shape, chosen_shape), {5: 0, 6: 1}, GHOSTS,
            )
        else:
            places, paces, _, _ = call(
                last_kernel, "last", (lists, parity, count),
                (own, speeds, kicks, near, far, sources, moments),
                (whole_shape, whole_shape, sources_shape, moments_shape),
                {5: 2, 6: 3}, LEAVES,
            )
    return places, paces


def solution(mesh):
    split = P(("gx", "gy"))
    columns = P(None, ("gx", "gy"))
    return jax.shard_map(
        body,
        mesh=mesh,
        in_specs=(columns, columns, split, columns, columns, split, split),
        out_specs=(columns, columns),
        check_vma=False,
    )
```

```python
import jax
import jax.numpy as jnp
from jax import lax
from jax.experimental import pallas as pl
from jax.experimental.pallas import tpu as pltpu
from jax.sharding import PartitionSpec as P

SUBCYCLES = 4
LEAF = 128
LEAVES = 64
GHOSTS = 8
NEIGHBOURS = 8
POOL = LEAVES + 9 * GHOSTS
FEATURES = 32
SUMS = 16
GROUP = 16
UNROLL = 8
PLAIN_BELOW = 2000.0

soften_sq = 0.04
cutoff_sq = 9.0
time_step = 0.5

f32, bf16 = jnp.float32, jnp.bfloat16


def three_parts(value):
    first = value.astype(bf16).astype(f32)
    rest = value - first
    second = rest.astype(bf16).astype(f32)
    return first, second, (rest - second).astype(bf16).astype(f32)


def norm(record):
    square = record * record
    return square[0:1] + square[1:2] + square[2:3]


def norm_parts(record, more=0.0):
    return three_parts(norm(record) + more)


def with_row(parts, row):
    last = lax.broadcasted_iota(jnp.int32, parts.shape, 0) == 3
    return jnp.where(last, jnp.broadcast_to(row, parts.shape), parts)


def source_features(record):
    a, b, c = three_parts(record)
    n1, n2, n3 = norm_parts(record)
    one = jnp.ones_like(n1)
    zero = jnp.zeros((8, LEAF), f32)
    return jnp.concatenate(
        [
            with_row(a, n1),
            with_row(a, n2),
            with_row(b, n3),
            with_row(b, one),
            with_row(a, one),
            with_row(c, one),
            zero,
        ],
        axis=0,
    )


def target_features(record):
    a, b, c = three_parts(record * -2.0)
    n1, n2, n3 = norm_parts(record, soften_sq)
    one = jnp.ones_like(n1)
    zero = jnp.zeros((8, LEAF), f32)
    return jnp.concatenate(
        [
            with_row(a, one),
            with_row(b, one),
            with_row(a, one),
            with_row(b, n1),
            with_row(c, n2),
            with_row(a, n3),
            zero,
        ],
        axis=0,
    )


def moment_rows(record):
    mass = jnp.broadcast_to(record[3:4], record.shape)
    a, b, c = three_parts(with_row(record, jnp.ones((1, LEAF), f32)) * mass)
    return jnp.concatenate([a, b, c, jnp.zeros_like(a)], axis=0).astype(bf16)


def enter(sources, moments, slot, record):
    features = source_features(record)
    blank = jnp.zeros((LEAF - FEATURES, LEAF), f32)
    sources[slot] = jnp.concatenate([features, blank], axis=0).T.astype(bf16)
    moments[slot] = moment_rows(record)
    return norm(record)


def enter_own(sources, moments, rows):
    def some(index, peak):
        for u in range(UNROLL):
            row = index * UNROLL + u
            peak = jnp.maximum(peak, enter(sources, moments, row, rows[row]))
        return peak

    return lax.fori_loop(0, LEAVES // UNROLL, some, jnp.zeros((1, LEAF), f32))


def is_plain(peak):
    return jnp.max(peak) < PLAIN_BELOW


def pair_sums(lists, sources, moments, leaves, records, plain):
    blank = jnp.zeros((FEATURES, LEAF), bf16)
    rest = jnp.zeros((LEAF - FEATURES, 2 * LEAF), bf16)
    first, second = (target_features(r).astype(bf16) for r in records)
    targets = jnp.concatenate(
        [
            jnp.concatenate([first, blank], axis=1),
            rest,
            jnp.concatenate([blank, second], axis=1),
            rest,
        ],
        axis=0,
    )
    slots = [[lists[n, leaf] for leaf in leaves] for n in range(NEIGHBOURS)]
    apart = jnp.dot(
        jnp.concatenate([jnp.concatenate([sources[s] for s in pair], axis=1) for pair in slots], axis=0),
        targets,
        preferred_element_type=f32,
    )
    weights, rows = [], []
    for n, pair in enumerate(slots):
        near = jnp.minimum(apart[n * LEAF : (n + 1) * LEAF], cutoff_sq + soften_sq)
        if not plain:
            near = jnp.maximum(near, soften_sq)
        taper = (cutoff_sq + soften_sq) - near
        inverse = lax.rsqrt(near)
        product = taper * inverse
        weight = product * product * inverse
        high = weight.astype(bf16)
        low = (weight - high.astype(f32)).astype(bf16)
        weights += [high, low]
        rows += [jnp.concatenate([moments[s] for s in pair], axis=0)] * 2
    total = jnp.dot(
        jnp.concatenate(rows, axis=1),
        jnp.concatenate(weights, axis=0),
        preferred_element_type=f32,
    )
    return total[:SUMS, :LEAF], total[SUMS:, LEAF:]


def moved(total, record, speed, kick):
    sums = (total[0:4] + total[4:8] + total[8:12]) * (1.0 / (cutoff_sq * cutoff_sq))
    accel = sums - record * jnp.broadcast_to(sums[3:4], sums.shape)
    row = lax.broadcasted_iota(jnp.int32, record.shape, 0)
    speed = jnp.where(row < 3, speed + time_step * (accel + kick), 0.0)
    return record + time_step * speed, speed


def group_moved(lists, sources, moments, own, speeds, kicks, leaves, plain):
    records = [own[leaf] for leaf in leaves]
    totals = []
    for k in range(0, len(leaves), 2):
        totals += pair_sums(lists, sources, moments, leaves[k : k + 2], records[k : k + 2], plain)
    return [
        moved(total, record, speeds[leaf], kicks[leaf])
        for total, record, leaf in zip(totals, records, leaves)
    ]


def for_groups(plain, begin, end, size, move):
    def group(index, carry):
        move([index * size + u for u in range(size)], True)
        return carry

    def pair(index, carry):
        move([index * 2, index * 2 + 1], False)
        return carry

    begin, end = jnp.int32(begin), jnp.int32(end)
    halfway = jnp.where(plain, end, begin)
    lax.fori_loop(begin, halfway, group, 0)
    lax.fori_loop(halfway * (size // 2), end * (size // 2), pair, 0)


def move_groups(
    lists, count, peak, sources, moments, own, speeds, kicks, new_own, new_speeds, begin, end
):
    def move(leaves, plain):
        results = group_moved(lists, sources, moments, own, speeds, kicks, leaves, plain)
        for leaf, (record, speed) in zip(leaves, results):
            live = leaf < count[0]
            new_own[leaf] = jnp.where(live, record, own[leaf])
            new_speeds[leaf] = jnp.where(live, speed, speeds[leaf])

    for_groups(is_plain(peak[...]), begin, end, GROUP, move)


def lanes(leaf):
    return pl.ds(pl.multiple_of(leaf * LEAF, LEAF), LEAF)


def first_record(positions, masses, leaf):
    return jnp.concatenate([positions[:, lanes(leaf)], masses[:, lanes(leaf)]], axis=0)


def choose_kernel(ids, positions, masses, chosen):
    for g in range(GHOSTS):
        chosen[g] = first_record(positions, masses, ids[g])


def open_kernel(
    positions, velocities, masses, long_kick, own, speeds, kicks, sources, moments, peak
):
    blank = jnp.zeros((1, LEAF), f32)

    def some(index, highest):
        for u in range(UNROLL):
            leaf = index * UNROLL + u
            record = first_record(positions, masses, leaf)
            own[leaf] = record
            speeds[leaf] = jnp.concatenate([velocities[:, lanes(leaf)], blank], axis=0)
            kicks[leaf] = jnp.concatenate([long_kick[:, lanes(leaf)], blank], axis=0)
            highest = jnp.maximum(highest, enter(sources, moments, leaf, record))
        return highest

    peak[...] = lax.fori_loop(0, LEAVES // UNROLL, some, blank)


def enter_ghosts(parity, sides, sources, moments, highest):
    for q, side in sides.items():
        b = jnp.where(parity[1] == 1, q, 2 - q)
        for p in range(3):
            a = jnp.where(parity[0] == 1, p, 2 - p)
            for g in range(GHOSTS):
                slot = LEAVES + (a * 3 + b) * GHOSTS + g
                highest = jnp.maximum(
                    highest, enter(sources, moments, slot, side[p * GHOSTS + g])
                )
    return highest


def ghost_kernel(
    lists, ids, parity, own, speeds, kicks, near, far, old_peak, old_sources, old_moments,
    sources, moments, chosen, peak,
):
    peak[...] = enter_ghosts(parity, {0: near, 2: far}, sources, moments, old_peak[...])

    def move(places, plain):
        leaves = [ids[g] for g in places]
        results = group_moved(lists, sources, moments, own, speeds, kicks, leaves, plain)
        for g, (record, _) in zip(places, results):
            chosen[g] = record

    for_groups(is_plain(peak[...]), 0, 1, GHOSTS, move)


def groups_of(count):
    return lax.div(count[0] + (GROUP - 1), GROUP)


def early_kernel(
    lists, count, own, speeds, kicks, peak, sources, moments, new_own, new_speeds
):
    move_groups(
        lists, count, peak, sources, moments, own, speeds, kicks, new_own, new_speeds,
        0, lax.div(groups_of(count), 2),
    )


def middle_kernel(parity, middle, old_peak, old_sources, old_moments, sources, moments, peak):
    peak[...] = enter_ghosts(parity, {1: middle}, sources, moments, old_peak[...])


def late_kernel(
    lists, parity, count, own, speeds, kicks, middle, old_peak, old_sources, old_moments,
    new_own, new_speeds, sources, moments, peak,
):
    groups = groups_of(count)
    move_groups(
        lists, count, old_peak, sources, moments, own, speeds, kicks, new_own, new_speeds,
        lax.div(groups, 2), groups,
    )
    highest = enter_own(sources, moments, new_own)
    peak[...] = enter_ghosts(parity, {1: middle}, sources, moments, highest)


def last_kernel(
    lists, parity, count, own, speeds, kicks, near, far, old_peak, old_sources, old_moments,
    places, paces, sources, moments,
):
    highest = enter_ghosts(parity, {0: near, 2: far}, sources, moments, old_peak[...])

    def move(leaves, plain):
        results = group_moved(lists, sources, moments, own, speeds, kicks, leaves, plain)
        for leaf, (record, speed) in zip(leaves, results):
            live = leaf < count[0]
            places[:, lanes(leaf)] = jnp.where(live, record, own[leaf])[:3]
            paces[:, lanes(leaf)] = jnp.where(live, speed, speeds[leaf])[:3]

    def keep(leaf, carry):
        places[:, lanes(leaf)] = own[leaf][:3]
        paces[:, lanes(leaf)] = speeds[leaf][:3]
        return carry

    groups = groups_of(count)
    for_groups(is_plain(highest), 0, groups, GROUP, move)
    lax.fori_loop(groups * GROUP, LEAVES, keep, 0)


VMEM = pl.BlockSpec(memory_space=pltpu.VMEM)
SMEM = pl.BlockSpec(memory_space=pltpu.SMEM)
record_shape = jax.ShapeDtypeStruct((LEAVES, 4, LEAF), f32)
whole_shape = jax.ShapeDtypeStruct((3, LEAVES * LEAF), f32)
peak_shape = jax.ShapeDtypeStruct((1, LEAF), f32)
chosen_shape = jax.ShapeDtypeStruct((GHOSTS, 4, LEAF), f32)
sources_shape = jax.ShapeDtypeStruct((POOL, LEAF, LEAF), bf16)
moments_shape = jax.ShapeDtypeStruct((POOL, SUMS, LEAF), bf16)


def call(kernel, name, scalars, arrays, outs, aliases=None, leaves=0):
    pairs = leaves * NEIGHBOURS * LEAF * LEAF
    return pl.pallas_call(
        kernel,
        out_shape=outs,
        in_specs=[SMEM] * len(scalars) + [VMEM] * len(arrays),
        out_specs=jax.tree.map(lambda _: VMEM, outs),
        input_output_aliases={len(scalars) + i: o for i, o in (aliases or {}).items()},
        compiler_params=pltpu.CompilerParams(vmem_limit_bytes=16 * 2**20),
        cost_estimate=pl.CostEstimate(
            flops=300 * pairs, bytes_accessed=2**20, transcendentals=pairs
        ),
        name=name,
    )(*scalars, *arrays)


def swapped(block, axis, odd):
    size = lax.axis_size(axis)
    route = []
    for i in range(odd, size + odd, 2):
        route += [(i % size, (i + 1) % size), ((i + 1) % size, i % size)]
    return lax.ppermute(block, axis, route)


def body(positions, velocities, masses, long_kick, leaf_lists, ghost_ids, leaf_counts):
    parity = jnp.stack([lax.axis_index("gx"), lax.axis_index("gy")]).astype(jnp.int32) % 2
    lists, ids, count = leaf_lists, ghost_ids, leaf_counts

    masses = masses[None]
    chosen = call(choose_kernel, "choose", (ids,), (positions, masses), chosen_shape)
    own, speeds, kicks, sources, moments, peak = call(
        open_kernel, "open", (), (positions, velocities, masses, long_kick),
        (record_shape,) * 3 + (sources_shape, moments_shape, peak_shape),
    )
    for subcycle in range(SUBCYCLES):
        far = swapped(chosen, "gx", 1)
        near = swapped(chosen, "gx", 0)
        if subcycle:
            own, speeds = call(
                early_kernel, "early", (lists, count),
                (own, speeds, kicks, peak, sources, moments),
                (record_shape, record_shape), {0: 0, 1: 1}, LEAVES // 2,
            )
        middle = jnp.concatenate([near, chosen, far], axis=0)
        if not subcycle:
            middle, own = lax.optimization_barrier((middle, own))
        far = swapped(middle, "gy", 1)
        near = swapped(middle, "gy", 0)
        if subcycle:
            own, speeds, sources, moments, peak = call(
                late_kernel, "late", (lists, parity, count),
                (own, speeds, kicks, middle, peak, sources, moments),
                (record_shape, record_shape, sources_shape, moments_shape, peak_shape),
                {0: 0, 1: 1, 5: 2, 6: 3}, LEAVES // 2,
            )
        else:
            sources, moments, peak = call(
                middle_kernel, "middle", (parity,), (middle, peak, sources, moments),
                (sources_shape, moments_shape, peak_shape), {2: 0, 3: 1}, 1,
            )
        if subcycle < SUBCYCLES - 1:
            sources, moments, chosen, peak = call(
                ghost_kernel, "ghost", (lists, ids, parity),
                (own, speeds, kicks, near, far, peak, sources, moments),
                (sources_shape, moments_shape, chosen_shape, peak_shape), {6: 0, 7: 1}, GHOSTS,
            )
        else:
            places, paces, _, _ = call(
                last_kernel, "last", (lists, parity, count),
                (own, speeds, kicks, near, far, peak, sources, moments),
                (whole_shape, whole_shape, sources_shape, moments_shape),
                {6: 2, 7: 3}, LEAVES,
            )
    return places, paces


def solution(mesh):
    split = P(("gx", "gy"))
    columns = P(None, ("gx", "gy"))
    return jax.shard_map(
        body,
        mesh=mesh,
        in_specs=(columns, columns, split, columns, columns, split, split),
        out_specs=(columns, columns),
        check_vma=False,
    )
```
